512 devices in a mesh: dp: 32 (over x, y, core), mp: 16 (over z).
Axes of the slice: x: 4, y: 4, z: 16, core: 2. Of those that a mesh axis runs over, the one named last changes fastest.
Arguments:
- activations: bfloat16 [4096, 8192], P('mp', 'dp'), may hold values from -600 to 600
- out_grads: bfloat16 [4096, 28672], P('dp', 'mp'), may hold values from -1 to 1
- row_moment: float32 [8192], P('dp'), may hold values from 0.003 to 0.3
- col_moment: float32 [28672], P('mp'), may hold values from 0.003 to 0.3
Outputs:
- update: float32 [8192, 28672], P('dp', 'mp')
- new_rows: float32 [8192], P('dp')
- new_cols: float32 [28672], P('mp')
The draws below stay inside these ranges and needn't reach their ends.
All inputs are finite; a program needn't handle non-finite values.
Results may differ from the reference program's by a relative error of at most 0.0003.
Values may be sent and summed in bfloat16 or wider, within the bound.
A program may use at most 64 MiB of HBM per device.

```python
import math
import jax
import jax.numpy as jnp
from jax import lax

D = 8192
F = 28672
TOKENS = 4096


def scaled_field(key, count, width, factor):
    first, second, third = jax.random.split(key, 3)
    ramp = jnp.arange(width, dtype=jnp.float32) / width
    wide_spread = jax.random.uniform(second, (width,), jnp.float32)
    narrow_spread = jax.random.uniform(third, (width,), jnp.float32)
    wide_scale = jnp.exp(wide_spread * math.log(30.0) + ramp * math.log(3.0))
    narrow_scale = 7.8 * jnp.exp(narrow_spread * math.log(2.0) + ramp * math.log(3.0))
    token_index = jnp.arange(count, dtype=jnp.int32)[:, None]
    column_scale = jnp.where(token_index < count // 2, wide_scale[None, :], narrow_scale[None, :])
    base = jnp.clip(jax.random.normal(first, (count, width), jnp.float32), -6.0, 6.0)
    return base * column_scale * factor


def draw_activations(key, part):
    key = jax.random.fold_in(key, 11)
    return scaled_field(key, TOKENS, D, 1.0).astype(jnp.bfloat16)


def draw_out_grads(key, part):
    key = jax.random.fold_in(key, 23)
    factor = 1.0 / (490.0 * math.sqrt(TOKENS))
    return scaled_field(key, TOKENS, F, factor).astype(jnp.bfloat16)


def block_levels(own_key, shape, cuts, smallest, largest):
    level, own = 1.0, jax.random.fold_in(own_key, 6)
    for dim, parts in cuts:
        heights = jnp.exp(jax.random.uniform(jax.random.fold_in(own, dim), (parts,), jnp.float32, smallest / len(cuts), largest / len(cuts)))
        level = level * jnp.repeat(heights, shape[dim] // parts).reshape([-1 if axis == dim else 1 for axis in range(len(shape))])
    return level


def setup_inputs(seed: int = 0) -> dict:
    keys = jax.random.split(jax.random.key(seed), 5)
    activations = draw_activations(jax.random.fold_in(keys[4], 71), 0)
    out_grads = draw_out_grads(jax.random.fold_in(keys[4], 71), 0)
    row_moment = jnp.clip(jnp.exp(math.log(0.3) - 4.6051702 * jax.random.uniform(keys[2], (D,), jnp.float32) ** block_levels(keys[2], (D,), ((0, 32),), -0.2, 0.2)), 0.003, 0.3)
    col_moment = jnp.clip(jnp.exp(math.log(0.3) - 4.6051702 * jax.random.uniform(keys[3], (F,), jnp.float32) ** block_levels(keys[3], (F,), ((0, 16),), -0.2, 0.2)), 0.003, 0.3)
    return {"activations": activations, "out_grads": out_grads, "row_moment": row_moment, "col_moment": col_moment}


decay_rate = 0.8
clip_bound = 1.0

def reference(activations, out_grads, row_moment, col_moment):
    gradient = jnp.dot(activations.T, out_grads, preferred_element_type=jnp.float32)
    squares = gradient * gradient
    new_rows = decay_rate * row_moment + (1.0 - decay_rate) * (lax.optimization_barrier(jnp.sum(squares, axis=1)) / F)
    new_cols = decay_rate * col_moment + (1.0 - decay_rate) * (lax.optimization_barrier(jnp.sum(squares, axis=0)) / D)
    scaled = gradient * lax.rsqrt(new_rows)[:, None] * lax.rsqrt(new_cols)[None, :]
    root_mean = jnp.sqrt(jnp.sum(scaled * scaled) / (D * F))
    update = scaled / jnp.maximum(1.0, root_mean / clip_bound)
    return (update, new_rows, new_cols)
```

```python
import functools

import jax
import jax.numpy as jnp
from jax import lax
from jax.experimental import pallas as pl
from jax.experimental.pallas import tpu as pltpu
from jax.sharding import PartitionSpec as P

decay_rate = 0.8
clip_bound = 1.0

MESH = pl.DeviceIdType.MESH
SIDE = 4
DEEP = 16
TILE = 256
PASSES = (2, 2, 2, 1)


def near(d):
    d = d % SIDE
    return d - SIDE if d == SIDE - 1 else d


def piece_names():
    names = []
    for half in range(2):
        for v in (0, -1, 1, 2):
            for u in (0, -1, 1, 2):
                if (u, v) == (0, 0):
                    continue
                last = u if v == 0 else v
                names += [(half, u, v, part) for part in (("a", "b") if last == 2 else ("f",))]
    return names


PIECES = {name: i for i, name in enumerate(piece_names())}


def exchange(
    act_ref, grad_ref, row_ref, col_ref,
    out_ref, rows_out, cols_out, clip_out,
    act, a_all, a_send, g_all, part, part_in, cols_mine, cols_core, cols_x, cols_y, cols_all, late, row_acc, z_all, clip_all,
    local_sem, a_send_sem, a_recv_sem, g_send_sem, g_recv_sem, core_send_sem, core_recv_sem,
    part_send_sem, part_recv_sem, x_send_sem, x_recv_sem, y_send_sem, y_recv_sem,
    late_send_sem, late_recv_sem, z_send_sem, z_recv_sem, clip_send_sem, clip_recv_sem,
):
    me, z = lax.axis_index("dp"), lax.axis_index("mp")
    x, y, core = me // 8, (me // 2) % SIDE, me % 2
    rows, tokens = act_ref.shape[1], grad_ref.shape[0]
    part_rows = tokens // 2
    tiles = sum(PASSES)
    early = sum(PASSES[:-1])

    def device(dx, dy, dc, dz):
        there = (((x + dx) % SIDE) * SIDE + (y + dy) % SIDE) * 2 + (core + dc) % 2
        return there, (z + dz) % DEEP

    def chip(dx, dy):
        return ((x + dx) % SIDE) * SIDE + (y + dy) % SIDE

    def remote(src, dst, send, recv, where):
        return pltpu.make_async_remote_copy(
            src_ref=src, dst_ref=dst, send_sem=send, recv_sem=recv,
            device_id=device(*where), device_id_type=MESH,
        )

    load_act = pltpu.make_async_copy(act_ref, act, local_sem.at[0])
    load_grad = pltpu.make_async_copy(grad_ref, g_all.at[chip(0, 0)], local_sem.at[1])
    load_grad.start()
    load_act.start()

    neighbours = [(1, 0, 0, 0), (-1, 0, 0, 0), (0, 1, 0, 0), (0, -1, 0, 0), (0, 0, 1, 0), (0, 0, 0, 1), (0, 0, 0, -1)]
    barrier = pltpu.get_barrier_semaphore()
    for where in neighbours:
        pl.semaphore_signal(barrier, inc=1, device_id=device(*where), device_id_type=MESH)
    load_grad.wait()
    pl.semaphore_wait(barrier, len(neighbours))

    starts = [sum(PASSES[:p]) * TILE for p in range(len(PASSES))]

    def g_piece(step, half, u, v, part_name):
        dx, dy = (u, v) if half == 0 else (v, u)
        offset, height = {"f": (0, part_rows), "a": (0, part_rows // 2), "b": (part_rows // 2, part_rows // 2)}[part_name]
        return g_all.at[
            chip(dx, dy),
            pl.ds(half * part_rows + offset, height),
            pl.ds(starts[step], PASSES[step] * TILE),
        ]

    def g_copy(step, half, u, v, part_name, axis, way):
        du, dv = (way, 0) if axis == 0 else (0, way)
        name = (half, near(u - du), near(v - dv), part_name)
        dx, dy = (du, dv) if half == 0 else (dv, du)
        ref = g_piece(step, half, u, v, part_name)
        return remote(ref, ref, g_send_sem, g_recv_sem.at[step, PIECES[name]], (dx, dy, 0, 0))

    def g_wait(step, half, u, v, part_name):
        ref = g_piece(step, half, u, v, part_name)
        pltpu.make_async_copy(ref, ref, g_recv_sem.at[step, PIECES[(half, u, v, part_name)]]).wait()

    def spread(step, half, u):
        for way in (1, -1):
            g_copy(step, half, u, 0, "f", 1, way).start()

    def own(step):
        def run():
            for half in range(2):
                for way in (1, -1):
                    g_copy(step, half, 0, 0, "f", 0, way).start()
            for half in range(2):
                spread(step, half, 0)

        return [run]

    def first(step):
        def run(half, u):
            g_wait(step, half, u, 0, "f")
            g_copy(step, half, u, 0, "a" if u < 0 else "b", 0, -u).start()
            spread(step, half, u)

        return [functools.partial(run, half, u) for u in (-1, 1) for half in range(2)]

    def opposite(step):
        def run(half):
            g_wait(step, half, 2, 0, "a")
            g_wait(step, half, 2, 0, "b")
            spread(step, half, 2)

        return [functools.partial(run, half) for half in range(2)]

    def second(step, u):
        def run(half, v):
            g_wait(step, half, u, v, "f")
            g_copy(step, half, u, v, "a" if v < 0 else "b", 1, -v).start()

        return [functools.partial(run, half, v) for v in (-1, 1) for half in range(2)]

    def final(step):
        def run(half, u):
            g_wait(step, half, u, 2, "a")
            g_wait(step, half, u, 2, "b")

        return [functools.partial(run, half, u) for u in (0, -1, 1, 2) for half in range(2)]

    def a_piece(kind, dz):
        owner = core if kind == 0 else 1 - core
        return a_all.at[owner, :, pl.ds(pl.multiple_of(((z + dz) % DEEP) * tokens, tokens), tokens)]

    def a_copy(kind, dz, way):
        ref = a_piece(kind, dz)
        return remote(ref, ref, a_send_sem, a_recv_sem.at[kind, (dz - way) % DEEP], (0, 0, 0, way))

    def a_reach(kind, way):
        return DEEP // 2 if (kind == 0) == (way == 1) else DEEP // 2 - 1

    def a_step(kind, way, far):
        dz = -way * far
        ref = a_piece(kind, dz)
        pltpu.make_async_copy(ref, ref, a_recv_sem.at[kind, dz % DEEP]).wait()
        if far < a_reach(kind, way):
            a_copy(kind, dz, way).start()

    def a_swap():
        return remote(
            a_send, a_all.at[core, :, pl.ds(pl.multiple_of(z * tokens, tokens), tokens)],
            core_send_sem.at[0], core_recv_sem.at[0], (0, 0, 1, 0),
        )

    def a_own():
        load_act.wait()
        turned = act[...].T
        lower, upper = turned[:, :tokens], turned[:, tokens:]
        a_all[core, :, pl.ds(pl.multiple_of(z * tokens, tokens), tokens)] = jnp.where(core == 0, lower, upper)
        a_send[...] = jnp.where(core == 0, upper, lower)
        a_swap().start()
        for way in (1, -1):
            a_copy(0, 0, way).start()

    def a_other():
        ref = a_piece(1, 0)
        pltpu.make_async_copy(ref, ref, core_recv_sem.at[0]).wait()
        for way in (1, -1):
            a_copy(1, 0, way).start()

    a_events = [a_own, a_other]
    for far in range(1, DEEP // 2 + 1):
        for kind in range(2):
            for way in (1, -1):
                if far <= a_reach(kind, way):
                    a_events.append(functools.partial(a_step, kind, way, far))

    def part_copy(t):
        return remote(part.at[t, 1 - core], part_in.at[t], part_send_sem.at[t], part_recv_sem.at[t], (0, 0, 1, 0))

    def product(t):
        left = a_all[...].reshape(2 * rows, DEEP * tokens)
        right = g_all[:, :, pl.ds(t * TILE, TILE)].reshape(DEEP * tokens, TILE)
        value = jnp.dot(left, right, preferred_element_type=jnp.float32)
        part[t] = value.reshape(2, rows, TILE)
        part_copy(t).start()

    def squares(t):
        block = out_ref[:, pl.ds(t * TILE, TILE)]
        return block * block

    def lanes(block):
        return sum(block[:, i * 128 : (i + 1) * 128] for i in range(TILE // 128))

    def joined(t):
        part_copy(t).wait_recv()
        out_ref[:, pl.ds(t * TILE, TILE)] = part[t, core] + part_in[t]
        square = squares(t)
        if t == 0:
            row_acc[0] = lanes(square)
        else:
            row_acc[0] = row_acc[0] + lanes(square)
        total = jnp.sum(square, axis=0, keepdims=True)
        if t < early:
            cols_mine[:, pl.ds(t * TILE, TILE)] = total
        else:
            late[me] = total

    def core_copy():
        return remote(cols_mine, cols_core, core_send_sem.at[1], core_recv_sem.at[1], (0, 0, 1, 0))

    def x_copy(k):
        return remote(cols_x.at[x], cols_x.at[x], x_send_sem.at[k], x_recv_sem.at[k], (k, 0, 0, 0))

    def x_wait(k):
        ref = cols_x.at[(x - k) % SIDE]
        pltpu.make_async_copy(ref, ref, x_recv_sem.at[k]).wait()

    def y_copy(k):
        return remote(cols_y.at[y], cols_y.at[y], y_send_sem.at[k], y_recv_sem.at[k], (0, k, 0, 0))

    def y_wait(k):
        ref = cols_y.at[(y - k) % SIDE]
        pltpu.make_async_copy(ref, ref, y_recv_sem.at[k]).wait()

    def cols_1():
        core_copy().start()

    def cols_2():
        core_copy().wait_recv()
        cols_x[x] = cols_mine[...] + cols_core[...]
        for k in (2, 1, 3):
            x_copy(k).start()

    def cols_3():
        for k in (1, 3, 2):
            x_wait(k)
        cols_y[y] = (cols_x[0] + cols_x[1]) + (cols_x[2] + cols_x[3])
        for k in (2, 1, 3):
            y_copy(k).start()

    def cols_4():
        for k in (1, 3, 2):
            y_wait(k)
        cols_all[:, pl.ds(0, early * TILE)] = (cols_y[0] + cols_y[1]) + (cols_y[2] + cols_y[3])

    last = len(PASSES) - 1
    order = []

    def put(events):
        for event in events:
            order.append(event)

    put(own(0))
    put([a_events.pop(0)])
    put(first(0))
    put(opposite(0))
    for step in range(last + 1):
        if step < last:
            put(own(step + 1))
        put(second(step, 0))
        put(second(step, -1))
        put(second(step, 1))
        if step < last:
            put(first(step + 1))
        put(second(step, 2))
        if step < last:
            put(opposite(step + 1))
        put(final(step))
        put([("pass", step)])

    count, ready, pending, chain = 0, [], [], [cols_1, cols_2, cols_3, cols_4]
    left_early = list(range(early))

    def join():
        t = pending.pop(0)
        joined(t)
        left_early.remove(t)

    def work():
        if a_events:
            return
        if ready and ready[0] < early:
            t = ready.pop(0)
            product(t)
            pending.append(t)
            if len(pending) > 1:
                join()
        elif pending:
            join()
        elif chain and not left_early:
            chain.pop(0)()

    for event in order:
        if isinstance(event, tuple):
            t0 = sum(PASSES[: event[1]])
            ready += range(t0, t0 + PASSES[event[1]])
            continue
        event()
        count += 1
        if a_events:
            if count % 2 == 0:
                a_events.pop(0)()
        elif count % 3 == 0:
            work()
    while a_events:
        a_events.pop(0)()
    while left_early:
        work()
    while len(chain) > 2:
        chain.pop(0)()
    for t in range(early, tiles):
        product(t)
    for t in range(early, tiles):
        joined(t)

    peers = [(dx, dy, dc) for dx in range(SIDE) for dy in range(SIDE) for dc in range(2) if (dx, dy, dc) != (0, 0, 0)]
    peers.sort(key=lambda p: -(min(p[0], SIDE - p[0]) + min(p[1], SIDE - p[1])))

    def from_peer(dx, dy, dc):
        return (((x - dx) % SIDE) * SIDE + (y - dy) % SIDE) * 2 + (core - dc) % 2

    def late_copy(i):
        return remote(late.at[me], late.at[me], late_send_sem.at[i], late_recv_sem.at[i], (*peers[i], 0))

    for i in range(len(peers)):
        late_copy(i).start()

    def flat(block):
        return jnp.sum(block.T, axis=0, keepdims=True)

    z_all[z, :, pl.ds(0, rows)] = flat(row_acc[0])
    while chain:
        chain.pop(0)()
    all_rows = rows * lax.axis_size("dp")
    all_cols = tiles * TILE * lax.axis_size("mp")

    def new_cols(t):
        span = pl.ds(t * TILE, TILE)
        return decay_rate * col_ref[:, span] + (1.0 - decay_rate) * (cols_all[:, span] / all_rows)

    for t in range(early):
        term = lanes(squares(t) * (1.0 / new_cols(t)))
        row_acc[1] = term if t == 0 else row_acc[1] + term
    for i, peer in enumerate(peers):
        ref = late.at[from_peer(*peer)]
        pltpu.make_async_copy(ref, ref, late_recv_sem.at[i]).wait()
    cols_all[:, pl.ds(early * TILE, (tiles - early) * TILE)] = jnp.sum(late[...], axis=0)
    for t in range(early, tiles):
        row_acc[1] = row_acc[1] + lanes(squares(t) * (1.0 / new_cols(t)))
    z_all[z, :, pl.ds(rows, rows)] = flat(row_acc[1])

    deep = sorted(range(1, DEEP), key=lambda k: -min(k, DEEP - k))

    def z_copy(i):
        return remote(z_all.at[z], z_all.at[z], z_send_sem.at[i], z_recv_sem.at[i], (0, 0, 0, deep[i]))

    for i in range(len(deep)):
        z_copy(i).start()
    cols_out[...] = cols_all[...]
    for i, k in enumerate(deep):
        ref = z_all.at[(z - k) % DEEP]
        pltpu.make_async_copy(ref, ref, z_recv_sem.at[i]).wait()
    sums = jnp.sum(z_all[...], axis=0)
    row_total = sums[:, :rows]
    new_rows = decay_rate * row_ref[...] + (1.0 - decay_rate) * (row_total / all_cols)
    share = sums[:, rows:] / new_rows
    clip_all[me] = sum(share[:, i * 128 : (i + 1) * 128] for i in range(rows // 128))

    def clip_copy(i):
        return remote(clip_all.at[me], clip_all.at[me], clip_send_sem.at[i], clip_recv_sem.at[i], (*peers[i], 0))

    for i in range(len(peers)):
        clip_copy(i).start()
    rows_out[...] = row_total
    sent = a_all.at[:, :, pl.ds(0, (DEEP - 1) * tokens)]
    pltpu.make_async_copy(sent, sent, a_send_sem).wait()
    sent = g_all.at[pl.ds(0, SIDE * SIDE - 1)]
    pltpu.make_async_copy(sent, sent, g_send_sem).wait()
    a_swap().wait_send()
    core_copy().wait_send()
    for k in range(1, SIDE):
        x_copy(k).wait_send()
        y_copy(k).wait_send()
    for t in range(tiles):
        part_copy(t).wait_send()
    for i in range(len(peers)):
        late_copy(i).wait_send()
    for i in range(len(deep)):
        z_copy(i).wait_send()
    for i, peer in enumerate(peers):
        ref = clip_all.at[from_peer(*peer)]
        pltpu.make_async_copy(ref, ref, clip_recv_sem.at[i]).wait()
    clip_out[...] = jnp.sum(clip_all[...], axis=0)
    for i in range(len(peers)):
        clip_copy(i).wait_send()


def finish(all_rows, all_cols, g_ref, rows_ref, cols_ref, clip_ref, row_ref, col_ref, out_ref, new_rows_ref, new_cols_ref, scale):
    rows = g_ref.shape[0]

    @pl.when(pl.program_id(0) == 0)
    def _():
        new_rows = decay_rate * row_ref[...] + (1.0 - decay_rate) * (rows_ref[...] / all_cols)
        new_rows_ref[...] = new_rows
        new_cols_ref[...] = decay_rate * col_ref[...] + (1.0 - decay_rate) * (cols_ref[...] / all_rows)
        total = jnp.sum(clip_ref[...], axis=1, keepdims=True)
        root_mean = jnp.sqrt(total / (all_rows * all_cols))
        factor = lax.rsqrt(new_rows) / jnp.maximum(1.0, root_mean / clip_bound)
        scale[...] = jnp.broadcast_to(factor, (128, rows)).T

    height = out_ref.shape[0]
    here = pl.ds(pl.multiple_of(pl.program_id(0) * height, height), height)
    weight = lax.rsqrt(new_cols_ref[...])
    for i in range(g_ref.shape[1] // 128):
        span = slice(i * 128, (i + 1) * 128)
        out_ref[:, span] = g_ref[here, span] * scale[here, :] * weight[:, span]


def shards(activations, out_grads, row_moment, col_moment):
    rows, tokens, columns = activations.shape[1], out_grads.shape[0], out_grads.shape[1]
    devices = lax.axis_size("dp")
    all_rows, all_cols = rows * devices, columns * lax.axis_size("mp")
    tiles = columns // TILE
    early = sum(PASSES[:-1]) * TILE
    f32, bf16 = jnp.float32, jnp.bfloat16
    vmem, anywhere = pl.BlockSpec(memory_space=pltpu.VMEM), pl.BlockSpec(memory_space=pl.ANY)
    dma = pltpu.SemaphoreType.DMA
    row_moment, col_moment = row_moment[None, :], col_moment[None, :]
    gradient, row_total, col_total, clip = pl.pallas_call(
        exchange,
        name="exchange",
        out_shape=(
            pltpu.VMEM((rows, columns), f32),
            jax.ShapeDtypeStruct((1, rows), f32),
            jax.ShapeDtypeStruct((1, columns), f32),
            jax.ShapeDtypeStruct((1, 128), f32),
        ),
        in_specs=[anywhere, anywhere, vmem, vmem],
        out_specs=(vmem,) * 4,
        scratch_shapes=[
            pltpu.VMEM((2 * tokens, rows), bf16),
            pltpu.VMEM((2, rows, DEEP * tokens), bf16),
            pltpu.VMEM((rows, tokens), bf16),
            pltpu.VMEM((SIDE * SIDE, tokens, columns), bf16),
            pltpu.VMEM((tiles, 2, rows, TILE), f32),
            pltpu.VMEM((tiles, rows, TILE), f32),
            pltpu.VMEM((1, early), f32),
            pltpu.VMEM((1, early), f32),
            pltpu.VMEM((SIDE, 1, early), f32),
            pltpu.VMEM((SIDE, 1, early), f32),
            pltpu.VMEM((1, columns), f32),
            pltpu.VMEM((devices, 1, columns - early), f32),
            pltpu.VMEM((2, rows, 128), f32),
            pltpu.VMEM((DEEP, 1, 2 * rows), f32),
            pltpu.VMEM((devices, 1, 128), f32),
            dma((2,)),
            dma,
            dma((2, DEEP)),
            dma,
            dma((len(PASSES), len(PIECES))),
            dma((2,)),
            dma((2,)),
            dma((tiles,)),
            dma((tiles,)),
            dma((SIDE,)),
            dma((SIDE,)),
            dma((SIDE,)),
            dma((SIDE,)),
            dma((devices - 1,)),
            dma((devices - 1,)),
            dma((DEEP - 1,)),
            dma((DEEP - 1,)),
            dma((devices - 1,)),
            dma((devices - 1,)),
        ],
        compiler_params=pltpu.CompilerParams(
            collective_id=0, has_side_effects=True, vmem_limit_bytes=40 << 20
        ),
        cost_estimate=pl.CostEstimate(
            flops=2 * rows * columns * tokens * devices, bytes_accessed=4 * rows * columns, transcendentals=0
        ),
    )(activations, out_grads, row_moment, col_moment)
    height = 64
    update, new_rows, new_cols = pl.pallas_call(
        functools.partial(finish, all_rows, all_cols),
        name="finish",
        grid=(rows // height,),
        out_shape=(
            jax.ShapeDtypeStruct((rows, columns), f32),
            jax.ShapeDtypeStruct((1, rows), f32),
            jax.ShapeDtypeStruct((1, columns), f32),
        ),
        in_specs=[vmem] * 6,
        out_specs=(pl.BlockSpec((height, columns), lambda i: (i, 0)), vmem, vmem),
        scratch_shapes=[pltpu.VMEM((rows, 128), f32)],
        compiler_params=pltpu.CompilerParams(vmem_limit_bytes=16 << 20),
    )(gradient, row_total, col_total, clip, row_moment, col_moment)
    return update, new_rows[0], new_cols[0]


def solution(mesh):
    placed = (P("mp", "dp"), P("dp", "mp"), P("dp"), P("mp"))
    return jax.shard_map(
        shards,
        mesh=mesh,
        in_specs=placed,
        out_specs=(P("dp", "mp"), P("dp"), P("mp")),
        check_vma=False,
    )
```
